256 devices in a mesh: ctx: 16 (over x, y_hi, core), tp: 16 (over y_lo, z).
Axes of the slice: x: 4, y: 4 (y_hi: 2, y_lo: 2; y = y_hi * 2 + y_lo), z: 8, core: 2. Of those that a mesh axis runs over, the one named last changes fastest.
Arguments:
- out_grad: bfloat16 [4096, 8192], P('ctx', 'tp'), may hold values from -6 to 6
- query_rows: bfloat16 [4096, 8192], P('ctx', 'tp'), may hold values from -6 to 6
- key_rows: bfloat16 [4096, 8192], P('ctx', 'tp'), may hold values from -6 to 6
- value_rows: bfloat16 [4096, 8192], P('ctx', 'tp'), may hold values from -6 to 6
- conv_rows: bfloat16 [4096, 8192], P('ctx', 'tp'), may hold values from -6 to 6
- long_filter: float32 [768, 8192], P('ctx', 'tp'), may hold values from -0.21650635 to 0.21650635
- block_table: int32 [32], replicated, may hold values from 0 to 31, each once
Outputs:
- q_grad: bfloat16 [4096, 8192], P('ctx', 'tp')
- k_grad: bfloat16 [4096, 8192], P('ctx', 'tp')
- v_grad: bfloat16 [4096, 8192], P('ctx', 'tp')
- filter_grad: float32 [768, 8192], P('ctx', 'tp')
The draws below stay inside these ranges and needn't reach their ends.
Inputs may be any that keep to these rules, and one draw needn't show every extreme that they name: slot s, block s % 2 of the device with index s // 2 along ctx, holds sequence block block_table[s]; every block appears once.
All inputs are finite; a program needn't handle non-finite values.
Results may differ from the reference program's by a relative error of at most 0.009.
Values may be sent and summed in bfloat16 or wider, within the bound.
A program may use at most 128 MiB of HBM per device.

```python
import math
import jax
import jax.numpy as jnp
from jax import lax

D = 8192
BLOCK = 128
LAG_BLOCKS = 6
SEQ = 4096
N_CTX = 16
N_TP = 16


def draw_long_filter(key, part):
    key = jax.random.fold_in(key, 11)
    noise_key, reach_key = jax.random.split(key)
    lag_total = LAG_BLOCKS * BLOCK
    position = jnp.arange(lag_total, dtype=jnp.float32)[:, None]
    amplitude = lag_total ** (-0.5)
    noise = jnp.clip(jax.random.normal(noise_key, (lag_total, D), jnp.float32), -6.0, 6.0)
    reach = jnp.exp(jax.random.uniform(reach_key, (1, D), jnp.float32, math.log(30.0), math.log(4.0 * lag_total)))
    return noise * jnp.exp(-position / reach) * amplitude


def steps_of(own_key, extent, pieces, smallest, high):
    factor_of, own = 1.0, jax.random.fold_in(own_key, 6)
    for dim, blocks in pieces:
        draws = jnp.exp(jax.random.uniform(jax.random.fold_in(own, dim), (blocks,), jnp.float32, smallest / len(pieces), high / len(pieces)))
        factor_of = factor_of * jnp.repeat(draws, extent[dim] // blocks).reshape([-1 if axis == dim else 1 for axis in range(len(extent))])
    return factor_of


def normal_values(key, shape, width, most, pieces=(), kind=jnp.bfloat16):
    entries = width * jax.random.normal(key, shape, jnp.float32)
    if pieces:
        entries = entries * steps_of(key, shape, pieces, -0.22, 0.18)
    return jnp.clip(entries, -most, most).astype(kind)


def setup_inputs(seed: int = 0) -> dict:
    streams_of = jax.random.split(jax.random.key(seed), 8)
    out_grad = normal_values(streams_of[0], (SEQ, D), 1.0, 6.0, ((0, 16), (1, 16)))
    query_rows = normal_values(streams_of[1], (SEQ, D), 1.0, 6.0, ((0, 16), (1, 16)))
    key_rows = normal_values(streams_of[2], (SEQ, D), 1.0, 6.0, ((0, 16), (1, 16)))
    value_rows = normal_values(streams_of[3], (SEQ, D), 1.0, 6.0, ((0, 16), (1, 16)))
    conv_rows = normal_values(streams_of[4], (SEQ, D), 1.0, 6.0, ((0, 16), (1, 16)))
    long_filter = draw_long_filter(jax.random.fold_in(streams_of[7], 71), 0)
    block_table = jax.random.permutation(streams_of[6], 2 * N_CTX).astype(jnp.int32)
    return {"out_grad": out_grad, "query_rows": query_rows, "key_rows": key_rows, "value_rows": value_rows, "conv_rows": conv_rows, "long_filter": long_filter, "block_table": block_table}


def to_sequence(slot_rows, block_table):
    columns = slot_rows.shape[1]
    blocks = slot_rows.reshape(2 * N_CTX, BLOCK, columns)
    ordered = jnp.zeros_like(blocks).at[block_table].set(blocks)
    return ordered.reshape(2 * N_CTX * BLOCK, columns)


def to_slots(seq_rows, block_table):
    columns = seq_rows.shape[1]
    blocks = seq_rows.reshape(2 * N_CTX, BLOCK, columns)
    return blocks[block_table].reshape(2 * N_CTX * BLOCK, columns)


def correlate(leading, trailing, lag_count):
    length = 2 * (leading.shape[0] + trailing.shape[0])
    spectrum = jnp.conj(jnp.fft.rfft(leading, n=length, axis=0)) * jnp.fft.rfft(trailing, n=length, axis=0)
    return jnp.fft.irfft(spectrum, n=length, axis=0)[:lag_count]


def group_grads(member):
    w_rows, u_rows, taps = member
    factor = (2.0 * N_CTX * BLOCK) ** -0.5
    seq_grad = correlate(taps, w_rows, 2 * N_CTX * BLOCK)
    filter_raw = correlate(u_rows, w_rows, LAG_BLOCKS * BLOCK) * factor
    return seq_grad, filter_raw


def rounded(values):
    low = lax.optimization_barrier(values.astype(jnp.bfloat16))
    return low.astype(jnp.float32)


def reference(out_grad, query_rows, key_rows, value_rows, conv_rows, long_filter, block_table):
    groups = N_TP
    col_group = D // N_TP

    def split_cols(rows):
        return rows.reshape(rows.shape[0], groups, col_group).transpose(1, 0, 2)

    def join_cols(stacked):
        return stacked.transpose(1, 0, 2).reshape(stacked.shape[1], groups * col_group)

    grad_f = out_grad.astype(jnp.float32)
    key_f = key_rows.astype(jnp.float32)
    value_f = value_rows.astype(jnp.float32)
    q_grad = (grad_f * conv_rows.astype(jnp.float32)).astype(jnp.bfloat16)
    weighted = rounded(grad_f * query_rows.astype(jnp.float32))
    product = rounded(key_f * value_f)
    w_seq = to_sequence(weighted, block_table)
    u_seq = to_sequence(product, block_table)
    seq_grad, filter_raw = lax.map(group_grads, (split_cols(w_seq), split_cols(u_seq), split_cols(long_filter)))
    seq_grad = to_slots(join_cols(seq_grad), block_table)
    filter_raw = join_cols(filter_raw)
    k_grad = (seq_grad * value_f).astype(jnp.bfloat16)
    v_grad = (seq_grad * key_f).astype(jnp.bfloat16)
    return q_grad, k_grad, v_grad, filter_raw
```

```python
import functools

import jax
import jax.numpy as jnp
import numpy as np
from jax import lax
from jax.experimental import pallas as pl
from jax.experimental.pallas import tpu as pltpu
from jax.sharding import PartitionSpec as P

BLOCK = 128
LAG_BLOCKS = 6
SPAN = 2 * BLOCK
RANKS = 16
SLOTS = 2 * RANKS
MESH = pl.DeviceIdType.MESH
F32 = jnp.float32
BF16 = jnp.bfloat16
NT = (((1,), (1,)), ((), ()))


def tables():
    time = np.arange(SPAN)[:, None]
    bins = np.arange(BLOCK)[None, :] + 0.5
    angles = 2.0 * np.pi * time * bins / SPAN
    forward = np.concatenate([np.cos(angles), -np.sin(angles)], 1)
    back = np.concatenate([np.cos(angles[:BLOCK]).T, -np.sin(angles[:BLOCK]).T], 0) * (2.0 / SPAN)
    return jnp.asarray(forward, BF16), jnp.asarray(back, BF16), jnp.asarray(np.eye(SPAN), BF16)


def dot(left, right):
    return jnp.dot(left, right, preferred_element_type=F32)


def flip(eye, rows):
    return lax.dot_general(eye, rows, NT, preferred_element_type=F32)


def peer(me, offset):
    dx, dy, dc = offset
    x = lax.rem(lax.div(me, 4) + dx, 4)
    y = lax.rem(lax.rem(lax.div(me, 2), 2) + dy, 2)
    c = lax.rem(lax.rem(me, 2) + dc, 2)
    return (x * 2 + y) * 2 + c


OFFSETS = sorted(
    [(dx, dy, dc) for dx in range(4) for dy in range(2) for dc in range(2)][1:],
    key=lambda o: -(min(o[0], 4 - o[0]) + 2 * o[1] + o[2]),
)


def exchange_kernel(
    table, grad, query, key, value, taps, forward, back, eye, out,
    inverse, send_a, recv_a, send_b, spec_v, spec_u, spec_h, spec_d, spec_f,
    a_send, a_recv, b_send, b_recv, own_sem,
):
    me = lax.axis_index("ctx")
    barrier = pltpu.get_barrier_semaphore()
    for offset in OFFSETS:
        pl.semaphore_signal(barrier, inc=1, device_id={"ctx": peer(me, offset)}, device_id_type=MESH)

    unit = eye[...]
    for which, (left, right) in enumerate(((grad, query), (key, value))):
        product = (left[...].astype(F32) * right[...].astype(F32)).astype(BF16)
        for half in range(2):
            turned = flip(unit, product[:, half * SPAN:(half + 1) * SPAN]).astype(BF16)
            for piece in range(8):
                rows = turned[piece * 32:(piece + 1) * 32]
                send_a[half * 8 + piece, 2 * which] = rows[:, :BLOCK]
                send_a[half * 8 + piece, 2 * which + 1] = rows[:, BLOCK:]
    lags = taps.shape[0]
    padded = jnp.concatenate([taps[...].astype(BF16), jnp.zeros((BLOCK - lags, taps.shape[1]), BF16)], 0)
    for half in range(2):
        turned = flip(unit, padded[:, half * SPAN:(half + 1) * SPAN]).astype(BF16)
        for piece in range(8):
            send_a[half * 8 + piece, 4] = turned[piece * 32:(piece + 1) * 32]

    pl.semaphore_wait(barrier, len(OFFSETS))
    copies = []
    for i, offset in enumerate(OFFSETS):
        to = peer(me, offset)
        copy = pltpu.make_async_remote_copy(
            send_a.at[to], recv_a.at[me], a_send.at[i], a_recv.at[i],
            device_id={"ctx": to}, device_id_type=MESH,
        )
        copy.start()
        copies.append(copy)
    own = pltpu.make_async_copy(send_a.at[me], recv_a.at[me], own_sem)
    own.start()

    def slot_of(p, carry):
        found = jnp.int32(0)
        for s in range(SLOTS):
            found = jnp.where(table[s] == p, s, found)
        inverse[p] = found
        return carry

    lax.fori_loop(0, SLOTS, slot_of, 0)
    own.wait()
    for copy in copies:
        copy.wait()

    lane = lax.broadcasted_iota(jnp.int32, (32, BLOCK), 1)
    order = [jnp.zeros((32, BLOCK), F32) for _ in range(LAG_BLOCKS)]
    for src in range(RANKS):
        first, shift = divmod(src * lags, BLOCK)
        rows = recv_a[src, 4].astype(F32)
        if shift:
            rows = pltpu.roll(rows, shift, 1)
        if shift + lags > BLOCK:
            order[first] = order[first] + jnp.where(lane >= shift, rows, 0.0)
            order[first + 1] = order[first + 1] + jnp.where(lane < shift, rows, 0.0)
        else:
            order[first] = order[first] + rows
    half_forward = forward[:BLOCK]
    spec_h[...] = dot(jnp.concatenate(order, 0).astype(BF16), half_forward).reshape(LAG_BLOCKS, 32, SPAN)

    full_forward = forward[...]
    chunk = 8
    for start in range(0, SLOTS, chunk):
        rows_w = []
        rows_u = []
        for p in range(start, start + chunk + 1):
            if p < SLOTS:
                slot = inverse[p]
                src = lax.div(slot, 2)
                b = lax.rem(slot, 2)
                rows_w.append(recv_a[src, b])
                if p < start + chunk:
                    rows_u.append(recv_a[src, 2 + b])
            else:
                rows_w.append(jnp.zeros((32, BLOCK), BF16))
        window = jnp.concatenate(
            [jnp.concatenate(rows_w[:-1], 0), jnp.concatenate(rows_w[1:], 0)], 1
        )
        spec_v[start:start + chunk] = dot(window, full_forward).reshape(chunk, 32, SPAN)
        spec_u[start:start + chunk] = dot(jnp.concatenate(rows_u, 0), half_forward).reshape(chunk, 32, SPAN)

    def group(g, carry):
        rows = pl.ds(pl.multiple_of(g * 8, 8), 8)
        h_re = [spec_h[m, rows, :BLOCK] for m in range(LAG_BLOCKS)]
        h_im = [spec_h[m, rows, BLOCK:] for m in range(LAG_BLOCKS)]
        f_re = [jnp.zeros((8, BLOCK), F32) for _ in range(LAG_BLOCKS)]
        f_im = [jnp.zeros((8, BLOCK), F32) for _ in range(LAG_BLOCKS)]
        for p in range(SLOTS):
            u_re, u_im = spec_u[p, rows, :BLOCK], spec_u[p, rows, BLOCK:]
            d_re = d_im = None
            for m in range(min(LAG_BLOCKS, SLOTS - p)):
                v_re, v_im = spec_v[p + m, rows, :BLOCK], spec_v[p + m, rows, BLOCK:]
                f_re[m] += u_re * v_re + u_im * v_im
                f_im[m] += u_re * v_im - u_im * v_re
                t_re = h_re[m] * v_re + h_im[m] * v_im
                t_im = h_re[m] * v_im - h_im[m] * v_re
                d_re = t_re if d_re is None else d_re + t_re
                d_im = t_im if d_im is None else d_im + t_im
            spec_d[p, rows, :BLOCK] = d_re
            spec_d[p, rows, BLOCK:] = d_im
        for m in range(LAG_BLOCKS):
            spec_f[m, rows, :BLOCK] = f_re[m]
            spec_f[m, rows, BLOCK:] = f_im[m]
        return carry

    lax.fori_loop(0, 4, group, 0)

    inverted = back[...]
    for start in range(0, SLOTS, chunk):
        rows_d = [spec_d[table[s]].astype(BF16) for s in range(start, start + chunk)]
        result = dot(jnp.concatenate(rows_d, 0), inverted).astype(BF16)
        for i in range(chunk):
            send_b[(start + i) // 2, (start + i) % 2] = result[i * 32:(i + 1) * 32]
    scale = float((SLOTS * BLOCK) ** -0.5)
    lagged = dot(spec_f[...].reshape(LAG_BLOCKS * 32, SPAN).astype(BF16), inverted) * scale
    for to in range(RANKS):
        first, shift = divmod(to * lags, BLOCK)
        rows = lagged[first * 32:(first + 1) * 32]
        if shift:
            rows = pltpu.roll(rows, BLOCK - shift, 1)
        if shift + lags > BLOCK:
            later = pltpu.roll(lagged[(first + 1) * 32:(first + 2) * 32], BLOCK - shift, 1)
            rows = jnp.where(lane < BLOCK - shift, rows, later)
        send_b[to, 2] = rows.astype(BF16)

    copies = []
    for i, offset in enumerate(OFFSETS):
        to = peer(me, offset)
        copy = pltpu.make_async_remote_copy(
            send_b.at[to], out.at[me], b_send.at[i], b_recv.at[i],
            device_id={"ctx": to}, device_id_type=MESH,
        )
        copy.start()
        copies.append(copy)
    own = pltpu.make_async_copy(send_b.at[me], out.at[me], own_sem)
    own.start()
    own.wait()
    for copy in copies:
        copy.wait()


def finish_kernel(grad, conv, key, value, eye, pieces, q_out, k_out, v_out, f_out):
    q_out[...] = (grad[...].astype(F32) * conv[...].astype(F32)).astype(BF16)
    unit = eye[:BLOCK, :BLOCK]
    channels = grad.shape[1]
    for b in range(2):
        rows = slice(b * BLOCK, (b + 1) * BLOCK)
        turned = flip(unit, pieces[:, b].reshape(channels, BLOCK))
        k_out[rows] = (turned * value[rows].astype(F32)).astype(BF16)
        v_out[rows] = (turned * key[rows].astype(F32)).astype(BF16)
    f_out[...] = flip(unit[:f_out.shape[0]], pieces[:, 2].reshape(channels, BLOCK))


def on_device(out_grad, query_rows, key_rows, value_rows, conv_rows, long_filter, block_table):
    forward, back, eye = tables()
    vmem = pl.BlockSpec(memory_space=pltpu.VMEM)
    units = (RANKS, 3, 32, BLOCK)
    dma = pltpu.SemaphoreType.DMA
    pieces = pl.pallas_call(
        exchange_kernel,
        name="exchange",
        out_shape=jax.ShapeDtypeStruct(units, BF16),
        in_specs=[pl.BlockSpec(memory_space=pltpu.SMEM)] + [vmem] * 8,
        out_specs=vmem,
        scratch_shapes=[
            pltpu.SMEM((SLOTS,), jnp.int32),
            pltpu.VMEM((RANKS, 5, 32, BLOCK), BF16),
            pltpu.VMEM((RANKS, 5, 32, BLOCK), BF16),
            pltpu.VMEM(units, BF16),
            pltpu.VMEM((SLOTS, 32, SPAN), F32),
            pltpu.VMEM((SLOTS, 32, SPAN), F32),
            pltpu.VMEM((LAG_BLOCKS, 32, SPAN), F32),
            pltpu.VMEM((SLOTS, 32, SPAN), F32),
            pltpu.VMEM((LAG_BLOCKS, 32, SPAN), F32),
            dma((15,)), dma((15,)), dma((15,)), dma((15,)), dma,
        ],
        compiler_params=pltpu.CompilerParams(
            collective_id=0, has_side_effects=True, vmem_limit_bytes=40 * 1024 * 1024
        ),
    )(block_table, out_grad, query_rows, key_rows, value_rows, long_filter, forward, back, eye)
    rows = jax.ShapeDtypeStruct(out_grad.shape, BF16)
    return pl.pallas_call(
        finish_kernel,
        name="finish",
        out_shape=(rows, rows, rows, jax.ShapeDtypeStruct(long_filter.shape, F32)),
        in_specs=[vmem] * 6,
        out_specs=[vmem] * 4,
        compiler_params=pltpu.CompilerParams(vmem_limit_bytes=40 * 1024 * 1024),
    )(out_grad, conv_rows, key_rows, value_rows, eye, pieces)


def solution(mesh):
    rows = P("ctx", "tp")
    return jax.shard_map(
        on_device, mesh=mesh, in_specs=(rows,) * 6 + (P(),), out_specs=(rows,) * 4, check_vma=False
    )
```

```python
import functools

import jax
import jax.numpy as jnp
import numpy as np
from jax import lax
from jax.experimental import pallas as pl
from jax.experimental.pallas import tpu as pltpu
from jax.sharding import PartitionSpec as P

BLOCK = 128
LAG_BLOCKS = 6
SPAN = 2 * BLOCK
RANKS = 16
SLOTS = 2 * RANKS
MESH = pl.DeviceIdType.MESH
F32 = jnp.float32
BF16 = jnp.bfloat16
NT = (((1,), (1,)), ((), ()))


def tables():
    time = np.arange(SPAN)[:, None]
    bins = np.arange(BLOCK)[None, :] + 0.5
    angles = 2.0 * np.pi * time * bins / SPAN
    forward = np.concatenate([np.cos(angles), -np.sin(angles)], 1)
    back = np.concatenate([np.cos(angles[:BLOCK]).T, -np.sin(angles[:BLOCK]).T], 0) * (2.0 / SPAN)
    return jnp.asarray(forward, BF16), jnp.asarray(back, BF16)


def dot(left, right):
    return jnp.dot(left, right, preferred_element_type=F32)


def flip(eye, rows):
    return lax.dot_general(eye, rows, NT, preferred_element_type=F32)


def peer(me, offset):
    dx, dy, dc = offset
    x = lax.rem(lax.div(me, 4) + dx, 4)
    y = lax.rem(lax.rem(lax.div(me, 2), 2) + dy, 2)
    c = lax.rem(lax.rem(me, 2) + dc, 2)
    return (x * 2 + y) * 2 + c


OFFSETS = sorted(
    [(dx, dy, dc) for dx in range(4) for dy in range(2) for dc in range(2)][1:],
    key=lambda o: -(min(o[0], 4 - o[0]) + 2 * o[1] + o[2]),
)


CHUNKS = 4
ROWS = 8


def load_all(pairs, sems):
    loads = []
    for i, (source, target) in enumerate(pairs):
        load = pltpu.make_async_copy(source, target, sems.at[i])
        load.start()
        loads.append(load)
    return loads


def unit_matrix(size):
    row = lax.broadcasted_iota(jnp.int32, (size, size), 0)
    column = lax.broadcasted_iota(jnp.int32, (size, size), 1)
    return jnp.where(row == column, 1.0, 0.0).astype(BF16)


def exchange_kernel(
    table_in, grad_in, query_in, key_in, value_in, taps_in, forward_in, back_in, out,
    table, inverse, grad, query, key, value, taps, forward, back,
    send_f, recv_f, send_a, recv_a, send_b, spec_w, spec_u, spec_h, spec_d, spec_f, lag_rows,
    load_sems, f_send, f_recv, a_send, a_recv, b_send, b_recv, own_sems,
):
    me = lax.axis_index("ctx")
    loads = load_all(
        ((taps_in, taps), (grad_in, grad), (query_in, query), (key_in, key), (value_in, value),
         (forward_in, forward), (back_in, back), (table_in, table)),
        load_sems,
    )
    peers = [peer(me, offset) for offset in OFFSETS]
    barrier = pltpu.get_barrier_semaphore()
    for to in peers:
        pl.semaphore_signal(barrier, inc=1, device_id={"ctx": to}, device_id_type=MESH)

    def send(source, target, send_sems, recv_sems):
        copies = []
        for i, to in enumerate(peers):
            copy = pltpu.make_async_remote_copy(
                source(to), target, send_sems.at[i], recv_sems.at[i],
                device_id={"ctx": to}, device_id_type=MESH,
            )
            copy.start()
            copies.append(copy)
        return copies

    unit = unit_matrix(SPAN)
    lane = lax.broadcasted_iota(jnp.int32, (16, BLOCK), 1)
    lower = lane < 64
    lags = taps.shape[0]
    loads[0].wait()
    padded = jnp.concatenate([taps[...].astype(BF16), jnp.zeros((BLOCK - lags, taps.shape[1]), BF16)], 0)
    for half in range(2):
        turned = flip(unit, padded[:, half * SPAN:(half + 1) * SPAN])
        for piece in range(8):
            rows = turned[piece * 32:(piece + 1) * 32]
            packed = jnp.where(lower, rows[:16], pltpu.roll(rows[16:], 64, 1))
            send_f[half * 8 + piece] = packed.astype(BF16)

    for which, (left, right) in enumerate(((grad, query), (key, value))):
        loads[1 + 2 * which].wait()
        loads[2 + 2 * which].wait()
        product = (left[...].astype(F32) * right[...].astype(F32)).astype(BF16)
        for half in range(2):
            turned = flip(unit, product[:, half * SPAN:(half + 1) * SPAN]).reshape(8, CHUNKS, ROWS, SPAN)
            for piece in range(8):
                for c in range(CHUNKS):
                    rows = turned[piece, c]
                    send_a[c, half * 8 + piece, which] = jnp.concatenate(
                        [rows[:, :BLOCK], rows[:, BLOCK:]], 0
                    ).astype(BF16)

    pl.semaphore_wait(barrier, len(OFFSETS))
    copies_f = send(lambda to: send_f.at[to], recv_f.at[me], f_send, f_recv)
    copies_a = [
        send(lambda to: send_a.at[c, to], recv_a.at[c, me], a_send.at[c], a_recv.at[c])
        for c in range(CHUNKS)
    ]
    own_f = pltpu.make_async_copy(send_f.at[me], recv_f.at[me], own_sems.at[0])
    own_f.start()
    own_a = pltpu.make_async_copy(send_a.at[:, me], recv_a.at[:, me], own_sems.at[1])
    own_a.start()

    def slot_of(p, carry):
        found = jnp.int32(0)
        for s in range(SLOTS):
            found = jnp.where(table[s] == p, s, found)
        inverse[p] = found
        return carry

    loads[7].wait()
    lax.fori_loop(0, SLOTS, slot_of, 0)
    own_f.wait()
    own_a.wait()
    loads[5].wait()
    loads[6].wait()

    for copy in copies_f:
        copy.wait_recv()
    order = [[jnp.zeros((16, BLOCK), F32) for _ in range(2)] for _ in range(LAG_BLOCKS)]
    for src in range(RANKS):
        first, shift = divmod(src * lags, BLOCK)
        packed = recv_f[src].astype(F32)
        for part in range(2):
            turn = (shift + 64 * part) % BLOCK
            rows = pltpu.roll(packed, turn, 1) if turn else packed
            inside = (lane >= shift) & (lane < shift + lags)
            order[first][part] = jnp.where(inside, rows, order[first][part])
            if shift + lags > BLOCK:
                order[first + 1][part] = jnp.where(lane < shift + lags - BLOCK, rows, order[first + 1][part])
    taps_in_order = jnp.concatenate([part for parts in order for part in parts], 0).astype(BF16)
    spec_h[...] = dot(taps_in_order, forward[:BLOCK]).reshape(LAG_BLOCKS, 32, SPAN)

    copies_b = []
    for c in range(CHUNKS):
        for copy in copies_a[c]:
            copy.wait_recv()
        rows_w = recv_a[c, :, 0].reshape(RANKS * 2 * ROWS, BLOCK)
        rows_u = recv_a[c, :, 1].reshape(RANKS * 2 * ROWS, BLOCK)
        spec_w[:, :, :SPAN] = dot(rows_w, forward[:BLOCK]).reshape(SLOTS, ROWS, SPAN)
        spec_w[:, :, SPAN:] = dot(rows_w, forward[BLOCK:]).reshape(SLOTS, ROWS, SPAN)
        spec_u[...] = dot(rows_u, forward[:BLOCK]).reshape(SLOTS, ROWS, SPAN)

        def window(p):
            slot = inverse[p]
            re = spec_w[slot, :, :BLOCK]
            im = spec_w[slot, :, BLOCK:SPAN]
            if p + 1 < SLOTS:
                later = inverse[p + 1]
                re = re + spec_w[later, :, SPAN:SPAN + BLOCK]
                im = im + spec_w[later, :, SPAN + BLOCK:]
            return re, im

        group = slice(c * ROWS, (c + 1) * ROWS)
        h = [(spec_h[m, group, :BLOCK], spec_h[m, group, BLOCK:]) for m in range(LAG_BLOCKS)]
        f = [None] * LAG_BLOCKS
        windows = [window(p) for p in range(LAG_BLOCKS - 1)]
        for p in range(SLOTS):
            if p + LAG_BLOCKS - 1 < SLOTS:
                windows.append(window(p + LAG_BLOCKS - 1))
            slot = inverse[p]
            u_re, u_im = spec_u[slot, :, :BLOCK], spec_u[slot, :, BLOCK:]
            d = None
            for m in range(min(LAG_BLOCKS, SLOTS - p)):
                v_re, v_im = windows[p + m]
                h_re, h_im = h[m]
                term_f = (u_re * v_re + u_im * v_im, u_re * v_im - u_im * v_re)
                term_d = (h_re * v_re + h_im * v_im, h_re * v_im - h_im * v_re)
                f[m] = term_f if f[m] is None else (f[m][0] + term_f[0], f[m][1] + term_f[1])
                d = term_d if d is None else (d[0] + term_d[0], d[1] + term_d[1])
            windows[p] = None
            spec_d[p, :, :BLOCK] = d[0]
            spec_d[p, :, BLOCK:] = d[1]
        for m in range(LAG_BLOCKS):
            spec_f[m, :, :BLOCK] = f[m][0]
            spec_f[m, :, BLOCK:] = f[m][1]

        rows_d = jnp.concatenate([spec_d[table[s]] for s in range(SLOTS)], 0).astype(BF16)
        send_b[c] = dot(rows_d, back[...]).astype(BF16).reshape(RANKS, 2 * ROWS, BLOCK)
        copies_b += send(lambda to: send_b.at[c, to], out.at[c, me], b_send.at[c], b_recv.at[c])
        rows_f = spec_f[...].reshape(LAG_BLOCKS * ROWS, SPAN).astype(BF16)
        lag_rows[:, group] = dot(rows_f, back[...]).reshape(LAG_BLOCKS, ROWS, BLOCK)

    scale = float((SLOTS * BLOCK) ** -0.5)
    for to in range(RANKS):
        first, shift = divmod(to * lags, BLOCK)
        parts = []
        for part in range(2):
            turn = (64 * part - shift) % BLOCK
            rows = lag_rows[first, part * 16:(part + 1) * 16]
            rows = pltpu.roll(rows, turn, 1) if turn else rows
            if shift + lags > BLOCK:
                later = pltpu.roll(lag_rows[first + 1, part * 16:(part + 1) * 16], turn, 1)
                rows = jnp.where((lane & 63) < BLOCK - shift, rows, later)
            parts.append(rows)
        send_b[CHUNKS, to] = (jnp.where(lower, parts[0], parts[1]) * scale).astype(BF16)
    copies_b += send(
        lambda to: send_b.at[CHUNKS, to], out.at[CHUNKS, me], b_send.at[CHUNKS], b_recv.at[CHUNKS]
    )
    own_b = pltpu.make_async_copy(send_b.at[:, me], out.at[:, me], own_sems.at[0])
    own_b.start()
    own_b.wait()
    for copies in [copies_f] + copies_a:
        for copy in copies:
            copy.wait_send()
    for copy in copies_b:
        copy.wait()


def finish_kernel(grad, conv, key, value, pieces, q_out, k_out, v_out, f_out):
    q_out[...] = (grad[...].astype(F32) * conv[...].astype(F32)).astype(BF16)
    unit = unit_matrix(BLOCK)
    channels = grad.shape[1]
    chunks = pieces[:CHUNKS].astype(F32).reshape(CHUNKS, RANKS, 2, ROWS, BLOCK)
    for b in range(2):
        rows = slice(b * BLOCK, (b + 1) * BLOCK)
        piece = jnp.stack([chunks[c, :, b] for c in range(CHUNKS)], 1)
        turned = flip(unit, piece.reshape(channels, BLOCK).astype(BF16))
        k_out[rows] = (turned * value[rows].astype(F32)).astype(BF16)
        v_out[rows] = (turned * key[rows].astype(F32)).astype(BF16)
    packed = pieces[CHUNKS].astype(F32).reshape(RANKS * 16, BLOCK)
    upper = pltpu.roll(packed, 64, 1).reshape(RANKS, 16, BLOCK)
    both = jnp.stack([packed.reshape(RANKS, 16, BLOCK), upper], 1)
    f_out[...] = flip(unit[:f_out.shape[0]], both.reshape(channels, BLOCK).astype(BF16))


def on_device(out_grad, query_rows, key_rows, value_rows, conv_rows, long_filter, block_table):
    forward, back = tables()
    vmem = pl.BlockSpec(memory_space=pltpu.VMEM)
    units = (CHUNKS + 1, RANKS, 16, BLOCK)
    sums = pltpu.VMEM((LAG_BLOCKS, ROWS, SPAN), F32)
    dma = pltpu.SemaphoreType.DMA
    rows = jax.ShapeDtypeStruct(out_grad.shape, BF16)
    operands = (block_table, out_grad, query_rows, key_rows, value_rows, long_filter, forward, back)
    pieces = pl.pallas_call(
        exchange_kernel,
        name="exchange",
        out_shape=jax.ShapeDtypeStruct(units, BF16),
        in_specs=[pl.BlockSpec(memory_space=pltpu.HBM)] * 8,
        out_specs=vmem,
        scratch_shapes=[
            pltpu.SMEM((SLOTS,), jnp.int32),
            pltpu.SMEM((SLOTS,), jnp.int32),
            pltpu.VMEM(rows.shape, BF16),
            pltpu.VMEM(rows.shape, BF16),
            pltpu.VMEM(rows.shape, BF16),
            pltpu.VMEM(rows.shape, BF16),
            pltpu.VMEM(long_filter.shape, F32),
            pltpu.VMEM(forward.shape, BF16),
            pltpu.VMEM(back.shape, BF16),
            pltpu.VMEM((RANKS, 16, BLOCK), BF16),
            pltpu.VMEM((RANKS, 16, BLOCK), BF16),
            pltpu.VMEM((CHUNKS, RANKS, 2, 16, BLOCK), BF16),
            pltpu.VMEM((CHUNKS, RANKS, 2, 16, BLOCK), BF16),
            pltpu.VMEM(units, BF16),
            pltpu.VMEM((SLOTS, ROWS, 2 * SPAN), F32),
            pltpu.VMEM((SLOTS, ROWS, SPAN), F32),
            pltpu.VMEM((LAG_BLOCKS, 32, SPAN), F32),
            pltpu.VMEM((SLOTS, ROWS, SPAN), F32),
            sums,
            pltpu.VMEM((LAG_BLOCKS, 32, BLOCK), F32),
            dma((8,)), dma((15,)), dma((15,)), dma((CHUNKS, 15)), dma((CHUNKS, 15)),
            dma((CHUNKS + 1, 15)), dma((CHUNKS + 1, 15)), dma((2,)),
        ],
        compiler_params=pltpu.CompilerParams(
            collective_id=0, has_side_effects=True, vmem_limit_bytes=40 * 1024 * 1024
        ),
    )(*(pltpu.with_memory_space_constraint(x, pltpu.HBM) for x in operands))
    return pl.pallas_call(
        finish_kernel,
        name="finish",
        out_shape=(rows, rows, rows, jax.ShapeDtypeStruct(long_filter.shape, F32)),
        in_specs=[vmem] * 5,
        out_specs=[vmem] * 4,
        compiler_params=pltpu.CompilerParams(vmem_limit_bytes=40 * 1024 * 1024),
    )(out_grad, conv_rows, key_rows, value_rows, pieces)


def solution(mesh):
    rows = P("ctx", "tp")
    return jax.shard_map(
        on_device, mesh=mesh, in_specs=(rows,) * 6 + (P(),), out_specs=(rows,) * 4, check_vma=False
    )
```

```python
import functools

import jax
import jax.numpy as jnp
import numpy as np
from jax import lax
from jax.experimental import pallas as pl
from jax.experimental.pallas import tpu as pltpu
from jax.sharding import PartitionSpec as P

BLOCK = 128
LAG_BLOCKS = 6
SPAN = 2 * BLOCK
RANKS = 16
SLOTS = 2 * RANKS
MESH = pl.DeviceIdType.MESH
F32 = jnp.float32
BF16 = jnp.bfloat16
NT = (((1,), (1,)), ((), ()))


def tables():
    time = np.arange(SPAN)[:, None]
    bins = np.arange(BLOCK)[None, :] + 0.5
    angles = 2.0 * np.pi * time * bins / SPAN
    forward = np.concatenate([np.cos(angles), -np.sin(angles)], 1)
    back = np.concatenate([np.cos(angles[:BLOCK]).T, -np.sin(angles[:BLOCK]).T], 0) * (2.0 / SPAN)
    return jnp.asarray(forward, BF16), jnp.asarray(back, BF16)


def dot(left, right):
    return jnp.dot(left, right, preferred_element_type=F32)


def flip(eye, rows):
    return lax.dot_general(eye, rows, NT, preferred_element_type=F32)


def peer(me, offset):
    dx, dy, dc = offset
    x = lax.rem(lax.div(me, 4) + dx, 4)
    y = lax.rem(lax.rem(lax.div(me, 2), 2) + dy, 2)
    c = lax.rem(lax.rem(me, 2) + dc, 2)
    return (x * 2 + y) * 2 + c


OFFSETS = (
    (2, 1, 1), (2, 1, 0), (1, 1, 1), (3, 1, 0), (3, 1, 1), (1, 1, 0), (2, 0, 1), (0, 1, 0),
    (0, 1, 1), (2, 0, 0), (1, 0, 1), (3, 0, 0), (3, 0, 1), (1, 0, 0), (0, 0, 1),
)


CHUNKS = 4
ROWS = 8


def load_all(pairs, sems):
    loads = []
    for i, (source, target) in enumerate(pairs):
        load = pltpu.make_async_copy(source, target, sems.at[i])
        load.start()
        loads.append(load)
    return loads


def unit_matrix(size):
    row = lax.broadcasted_iota(jnp.int32, (size, size), 0)
    column = lax.broadcasted_iota(jnp.int32, (size, size), 1)
    return jnp.where(row == column, 1.0, 0.0).astype(BF16)


def exchange_kernel(
    table_in, grad_in, query_in, key_in, value_in, taps_in, forward_in, back_in, out,
    table, inverse, grad, query, key, value, taps, forward, back,
    send_w, recv_w, send_u, recv_u, send_b, spec_w, spec_v, spec_u, spec_h, spec_d, spec_f,
    load_sems, w_send, w_recv, u_send, u_recv, d_send, d_recv, f_send, f_recv, own_sems,
):
    me = lax.axis_index("ctx")
    loads = load_all(
        ((taps_in, taps), (grad_in, grad), (query_in, query), (key_in, key), (value_in, value),
         (forward_in, forward), (back_in, back), (table_in, table)),
        load_sems,
    )
    peers = [peer(me, offset) for offset in OFFSETS]
    barrier = pltpu.get_barrier_semaphore()
    for to in peers:
        pl.semaphore_signal(barrier, inc=1, device_id={"ctx": to}, device_id_type=MESH)

    def send(source, target, send_sems, recv_sems):
        copies = []
        for i, to in enumerate(peers):
            copy = pltpu.make_async_remote_copy(
                source(to), target, send_sems.at[i], recv_sems.at[i],
                device_id={"ctx": to}, device_id_type=MESH,
            )
            copy.start()
            copies.append(copy)
        return copies

    def keep(source, target, i):
        copy = pltpu.make_async_copy(source, target, own_sems.at[i])
        copy.start()
        return copy

    unit = unit_matrix(SPAN)
    lane = lax.broadcasted_iota(jnp.int32, (16, BLOCK), 1)
    lower = lane < 64
    lags = taps.shape[0]
    loads[0].wait()
    padded = jnp.concatenate([taps[...].astype(BF16), jnp.zeros((BLOCK - lags, taps.shape[1]), BF16)], 0)
    for half in range(2):
        turned = flip(unit, padded[:, half * SPAN:(half + 1) * SPAN])
        for piece in range(8):
            rows = turned[piece * 32:(piece + 1) * 32]
            packed = jnp.where(lower, rows[:16], pltpu.roll(rows[16:], 64, 1))
            send_w[half * 8 + piece, CHUNKS] = packed.astype(BF16)

    def cut(left, right, pieces):
        product = (left[...].astype(F32) * right[...].astype(F32)).astype(BF16)
        for half in range(2):
            turned = flip(unit, product[:, half * SPAN:(half + 1) * SPAN]).reshape(8, CHUNKS, ROWS, SPAN)
            for piece in range(8):
                for c in range(CHUNKS):
                    rows = turned[piece, c]
                    pieces[half * 8 + piece, c] = jnp.concatenate(
                        [rows[:, :BLOCK], rows[:, BLOCK:]], 0
                    ).astype(BF16)

    loads[1].wait()
    loads[2].wait()
    cut(grad, query, send_w)
    pl.semaphore_wait(barrier, len(OFFSETS))
    copies_w = send(lambda to: send_w.at[to], recv_w.at[me], w_send, w_recv)
    own_w = keep(send_w.at[me], recv_w.at[me], 0)
    loads[3].wait()
    loads[4].wait()
    cut(key, value, send_u)
    copies_u = send(lambda to: send_u.at[to], recv_u.at[me], u_send, u_recv)
    own_u = keep(send_u.at[me], recv_u.at[me], 1)

    def slot_of(p, carry):
        found = jnp.int32(0)
        for s in range(SLOTS):
            found = jnp.where(table[s] == p, s, found)
        inverse[p] = found
        return carry

    for load in loads[5:]:
        load.wait()
    lax.fori_loop(0, SLOTS, slot_of, 0)
    spec_v[:, SLOTS:] = jnp.zeros((CHUNKS, LAG_BLOCKS - 1, ROWS, SPAN), F32)
    spec_f[...] = jnp.zeros_like(spec_f)
    own_w.wait()
    own_u.wait()
    for copy in copies_w:
        copy.wait_recv()

    order = [[jnp.zeros((16, BLOCK), F32) for _ in range(2)] for _ in range(LAG_BLOCKS)]
    for src in range(RANKS):
        first, shift = divmod(src * lags, BLOCK)
        packed = recv_w[src, CHUNKS].astype(F32)
        for part in range(2):
            turn = (shift + 64 * part) % BLOCK
            rows = pltpu.roll(packed, turn, 1) if turn else packed
            inside = (lane >= shift) & (lane < shift + lags)
            order[first][part] = jnp.where(inside, rows, order[first][part])
            if shift + lags > BLOCK:
                order[first + 1][part] = jnp.where(lane < shift + lags - BLOCK, rows, order[first + 1][part])
    taps_in_order = jnp.concatenate([part for parts in order for part in parts], 0).astype(BF16)
    spec_h[...] = dot(taps_in_order, forward[:BLOCK]).reshape(LAG_BLOCKS, 32, SPAN)

    for c in range(CHUNKS):
        rows_w = recv_w[:, c].reshape(RANKS * 2 * ROWS, BLOCK)
        spec_w[c, :, :, :SPAN] = dot(rows_w, forward[:BLOCK]).reshape(SLOTS, ROWS, SPAN)
        spec_w[c, :, :, SPAN:] = dot(rows_w, forward[BLOCK:]).reshape(SLOTS, ROWS, SPAN)

    for c in range(CHUNKS):
        def window(p):
            slot = inverse[p]
            re = spec_w[c, slot, :, :BLOCK]
            im = spec_w[c, slot, :, BLOCK:SPAN]
            if p + 1 < SLOTS:
                later = inverse[p + 1]
                re = re + spec_w[c, later, :, SPAN:SPAN + BLOCK]
                im = im + spec_w[c, later, :, SPAN + BLOCK:]
            spec_v[c, p, :, :BLOCK] = re
            spec_v[c, p, :, BLOCK:] = im
            return re, im

        group = slice(c * ROWS, (c + 1) * ROWS)
        h = [(spec_h[m, group, :BLOCK], spec_h[m, group, BLOCK:]) for m in range(LAG_BLOCKS)]
        windows = [window(p) for p in range(LAG_BLOCKS - 1)]
        for p in range(SLOTS):
            if p + LAG_BLOCKS - 1 < SLOTS:
                windows.append(window(p + LAG_BLOCKS - 1))
            d = None
            for m in range(min(LAG_BLOCKS, SLOTS - p)):
                v_re, v_im = windows[p + m]
                h_re, h_im = h[m]
                term = (h_re * v_re + h_im * v_im, h_re * v_im - h_im * v_re)
                d = term if d is None else (d[0] + term[0], d[1] + term[1])
            windows[p] = None
            spec_d[c, p, :, :BLOCK] = d[0]
            spec_d[c, p, :, BLOCK:] = d[1]

        rows_d = jnp.concatenate([spec_d[c, table[s]] for s in range(SLOTS)], 0).astype(BF16)
        send_b[:, c] = dot(rows_d, back[...]).astype(BF16).reshape(RANKS, 2 * ROWS, BLOCK)
    copies_d = send(
        lambda to: send_b.at[to, pl.ds(0, CHUNKS)], out.at[me, pl.ds(0, CHUNKS)], d_send, d_recv
    )

    sources = [me] + [peer(me, ((4 - dx) % 4, dy, dc)) for dx, dy, dc in OFFSETS]
    for start in range(0, RANKS, 4):
        for copy in copies_u[max(start - 1, 0):start + 3]:
            copy.wait_recv()
        batch = sources[start:start + 4]
        rows_u = jnp.concatenate([recv_u[src].reshape(CHUNKS * 16, BLOCK) for src in batch], 0)
        spec_u[...] = dot(rows_u, forward[:BLOCK]).reshape(4, CHUNKS, 2, ROWS, SPAN)
        for c in range(CHUNKS):
            f = [(spec_f[c, m, :, :BLOCK], spec_f[c, m, :, BLOCK:]) for m in range(LAG_BLOCKS)]
            for i, src in enumerate(batch):
                for b in range(2):
                    p = table[2 * src + b]
                    u_re, u_im = spec_u[i, c, b, :, :BLOCK], spec_u[i, c, b, :, BLOCK:]
                    for m in range(LAG_BLOCKS):
                        v_re, v_im = spec_v[c, p + m, :, :BLOCK], spec_v[c, p + m, :, BLOCK:]
                        f[m] = (
                            f[m][0] + (u_re * v_re + u_im * v_im),
                            f[m][1] + (u_re * v_im - u_im * v_re),
                        )
            for m in range(LAG_BLOCKS):
                spec_f[c, m, :, :BLOCK] = f[m][0]
                spec_f[c, m, :, BLOCK:] = f[m][1]
    rows_f = spec_f[...].reshape(CHUNKS * LAG_BLOCKS * ROWS, SPAN).astype(BF16)
    scale = float((SLOTS * BLOCK) ** -0.5)
    lagged = (dot(rows_f, back[...]) * scale).reshape(CHUNKS, LAG_BLOCKS, ROWS, BLOCK)
    lag_rows = [
        [jnp.concatenate([lagged[2 * part, m], lagged[2 * part + 1, m]], 0) for part in range(2)]
        for m in range(LAG_BLOCKS)
    ]
    for to in range(RANKS):
        first, shift = divmod(to * lags, BLOCK)
        parts = []
        for part in range(2):
            turn = (64 * part - shift) % BLOCK
            rows = lag_rows[first][part]
            rows = pltpu.roll(rows, turn, 1) if turn else rows
            if shift + lags > BLOCK:
                later = pltpu.roll(lag_rows[first + 1][part], turn, 1)
                rows = jnp.where((lane & 63) < BLOCK - shift, rows, later)
            parts.append(rows)
        send_b[to, CHUNKS] = jnp.where(lower, parts[0], parts[1]).astype(BF16)
    copies_f = send(lambda to: send_b.at[to, CHUNKS], out.at[me, CHUNKS], f_send, f_recv)
    own_b = keep(send_b.at[me], out.at[me], 0)
    for copy in copies_w + copies_u:
        copy.wait_send()
    own_b.wait()
    for copy in copies_d + copies_f:
        copy.wait()


def finish_kernel(grad, conv, key, value, pieces, q_out, k_out, v_out, f_out):
    q_out[...] = (grad[...].astype(F32) * conv[...].astype(F32)).astype(BF16)
    unit = unit_matrix(BLOCK)
    channels = grad.shape[1]
    chunks = pieces[:, :CHUNKS].astype(F32).reshape(RANKS, CHUNKS, 2, ROWS, BLOCK)
    for b in range(2):
        rows = slice(b * BLOCK, (b + 1) * BLOCK)
        turned = flip(unit, chunks[:, :, b].reshape(channels, BLOCK).astype(BF16))
        k_out[rows] = (turned * value[rows].astype(F32)).astype(BF16)
        v_out[rows] = (turned * key[rows].astype(F32)).astype(BF16)
    packed = pieces[:, CHUNKS].astype(F32).reshape(RANKS * 16, BLOCK)
    upper = pltpu.roll(packed, 64, 1).reshape(RANKS, 16, BLOCK)
    both = jnp.stack([packed.reshape(RANKS, 16, BLOCK), upper], 1)
    f_out[...] = flip(unit[:f_out.shape[0]], both.reshape(channels, BLOCK).astype(BF16))


def on_device(out_grad, query_rows, key_rows, value_rows, conv_rows, long_filter, block_table):
    forward, back = tables()
    vmem = pl.BlockSpec(memory_space=pltpu.VMEM)
    units = (RANKS, CHUNKS + 1, 16, BLOCK)
    pieces_u = pltpu.VMEM((RANKS, CHUNKS, 16, BLOCK), BF16)
    dma = pltpu.SemaphoreType.DMA
    rows = jax.ShapeDtypeStruct(out_grad.shape, BF16)
    operands = (block_table, out_grad, query_rows, key_rows, value_rows, long_filter, forward, back)
    pieces = pl.pallas_call(
        exchange_kernel,
        name="exchange",
        out_shape=jax.ShapeDtypeStruct(units, BF16),
        in_specs=[pl.BlockSpec(memory_space=pltpu.HBM)] * 8,
        out_specs=vmem,
        scratch_shapes=[
            pltpu.SMEM((SLOTS,), jnp.int32),
            pltpu.SMEM((SLOTS,), jnp.int32),
            pltpu.VMEM(rows.shape, BF16),
            pltpu.VMEM(rows.shape, BF16),
            pltpu.VMEM(rows.shape, BF16),
            pltpu.VMEM(rows.shape, BF16),
            pltpu.VMEM(long_filter.shape, F32),
            pltpu.VMEM(forward.shape, BF16),
            pltpu.VMEM(back.shape, BF16),
            pltpu.VMEM(units, BF16),
            pltpu.VMEM(units, BF16),
            pieces_u,
            pieces_u,
            pltpu.VMEM(units, BF16),
            pltpu.VMEM((CHUNKS, SLOTS, ROWS, 2 * SPAN), F32),
            pltpu.VMEM((CHUNKS, SLOTS + LAG_BLOCKS - 1, ROWS, SPAN), F32),
            pltpu.VMEM((4, CHUNKS, 2, ROWS, SPAN), F32),
            pltpu.VMEM((LAG_BLOCKS, 32, SPAN), F32),
            pltpu.VMEM((CHUNKS, SLOTS, ROWS, SPAN), F32),
            pltpu.VMEM((CHUNKS, LAG_BLOCKS, ROWS, SPAN), F32),
            dma((8,)),
        ]
        + [dma((len(OFFSETS),))] * 8
        + [dma((2,))],
        compiler_params=pltpu.CompilerParams(
            collective_id=0, has_side_effects=True, vmem_limit_bytes=40 * 1024 * 1024
        ),
    )(*(pltpu.with_memory_space_constraint(x, pltpu.HBM) for x in operands))
    return pl.pallas_call(
        finish_kernel,
        name="finish",
        out_shape=(rows, rows, rows, jax.ShapeDtypeStruct(long_filter.shape, F32)),
        in_specs=[vmem] * 5,
        out_specs=[vmem] * 4,
        compiler_params=pltpu.CompilerParams(vmem_limit_bytes=40 * 1024 * 1024),
    )(out_grad, conv_rows, key_rows, value_rows, pieces)


def solution(mesh):
    rows = P("ctx", "tp")
    return jax.shard_map(
        on_device, mesh=mesh, in_specs=(rows,) * 6 + (P(),), out_specs=(rows,) * 4, check_vma=False
    )
```

```python
import functools

import jax
import jax.numpy as jnp
import numpy as np
from jax import lax
from jax.experimental import pallas as pl
from jax.experimental.pallas import tpu as pltpu
from jax.sharding import PartitionSpec as P

BLOCK = 128
LAG_BLOCKS = 6
SPAN = 2 * BLOCK
RANKS = 16
SLOTS = 2 * RANKS
MESH = pl.DeviceIdType.MESH
F32 = jnp.float32
BF16 = jnp.bfloat16
NT = (((1,), (1,)), ((), ()))


def tables():
    time = np.arange(SPAN)[:, None]
    bins = np.arange(BLOCK)[None, :] + 0.5
    angles = 2.0 * np.pi * time * bins / SPAN
    forward = np.concatenate([np.cos(angles), -np.sin(angles)], 1)
    back = np.concatenate([np.cos(angles[:BLOCK]).T, -np.sin(angles[:BLOCK]).T], 0) * (2.0 / SPAN)
    return jnp.asarray(forward, BF16), jnp.asarray(back, BF16)


def dot(left, right):
    return jnp.dot(left, right, preferred_element_type=F32)


def flip(eye, rows):
    return lax.dot_general(eye, rows, NT, preferred_element_type=F32)


def peer(me, offset):
    dx, dy, dc = offset
    x = lax.rem(lax.div(me, 4) + dx, 4)
    y = lax.rem(lax.rem(lax.div(me, 2), 2) + dy, 2)
    c = lax.rem(lax.rem(me, 2) + dc, 2)
    return (x * 2 + y) * 2 + c


OFFSETS = (
    (2, 1, 1), (2, 1, 0), (1, 1, 1), (3, 1, 0), (3, 1, 1), (1, 1, 0), (2, 0, 1), (0, 1, 0),
    (0, 1, 1), (2, 0, 0), (1, 0, 1), (3, 0, 0), (3, 0, 1), (1, 0, 0), (0, 0, 1),
)


CHUNKS = 4
ROWS = 8
BATCHES = (4, 4, 4, 2, 2)
THIRDS = tuple(slice(i * BLOCK, (i + 1) * BLOCK) for i in range(3))


def load_all(pairs, sems):
    loads = []
    for i, (source, target) in enumerate(pairs):
        load = pltpu.make_async_copy(source, target, sems.at[i])
        load.start()
        loads.append(load)
    return loads


def unit_matrix(size):
    row = lax.broadcasted_iota(jnp.int32, (size, size), 0)
    column = lax.broadcasted_iota(jnp.int32, (size, size), 1)
    return jnp.where(row == column, 1.0, 0.0).astype(BF16)


def exchange_kernel(
    table_in, grad_in, query_in, key_in, value_in, conv_in, taps_in, forward_in, back_in, out, q_out,
    table, inverse, grad, query, key, value, conv, taps, forward, back,
    send_t, recv_t, send_w, recv_w, send_u, recv_u, send_b, spec_h, spec_u,
    spec_w0, spec_w1, spec_w2, spec_w3, spec_v0, spec_v1, spec_v2, spec_v3,
    spec_d0, spec_d1, spec_d2, spec_d3, spec_f0, spec_f1, spec_f2, spec_f3,
    load_sems, t_send, t_recv, w_send, w_recv, u_send, u_recv, d_send, d_recv, f_send, f_recv, own_sems,
):
    spec_w = (spec_w0, spec_w1, spec_w2, spec_w3)
    spec_v = (spec_v0, spec_v1, spec_v2, spec_v3)
    spec_d = (spec_d0, spec_d1, spec_d2, spec_d3)
    spec_f = (spec_f0, spec_f1, spec_f2, spec_f3)
    me = lax.axis_index("ctx")
    peers = [peer(me, offset) for offset in OFFSETS]
    barrier = pltpu.get_barrier_semaphore()
    for to in peers:
        pl.semaphore_signal(barrier, inc=1, device_id={"ctx": to}, device_id_type=MESH)
    sources = [me] + [peer(me, ((4 - dx) % 4, dy, dc)) for dx, dy, dc in OFFSETS]
    loads = load_all(
        ((taps_in, taps), (grad_in, grad), (query_in, query), (key_in, key), (value_in, value),
         (forward_in, forward), (back_in, back), (table_in, table), (conv_in, conv)),
        load_sems,
    )

    def send(source, target, send_sems, recv_sems):
        copies = []
        for i, to in enumerate(peers):
            copy = pltpu.make_async_remote_copy(
                source(to), target, send_sems.at[i], recv_sems.at[i],
                device_id={"ctx": to}, device_id_type=MESH,
            )
            copy.start()
            copies.append(copy)
        return copies

    def keep(source, target, i):
        copy = pltpu.make_async_copy(source, target, own_sems.at[i])
        copy.start()
        return copy

    unit = unit_matrix(SPAN)
    lane = lax.broadcasted_iota(jnp.int32, (16, BLOCK), 1)
    lower = lane < 64
    lags = taps.shape[0]
    loads[0].wait()
    padded = jnp.concatenate([taps[...].astype(BF16), jnp.zeros((BLOCK - lags, taps.shape[1]), BF16)], 0)
    for half in range(2):
        turned = flip(unit, padded[:, half * SPAN:(half + 1) * SPAN])
        for piece in range(8):
            rows = turned[piece * 32:(piece + 1) * 32]
            packed = jnp.where(lower, rows[:16], pltpu.roll(rows[16:], 64, 1))
            send_t[half * 8 + piece] = packed.astype(BF16)

    def cut(left, right, pieces):
        product = (left[...].astype(F32) * right[...].astype(F32)).astype(BF16)
        for half in range(2):
            turned = flip(unit, product[:, half * SPAN:(half + 1) * SPAN]).reshape(8, CHUNKS, ROWS, SPAN)
            for piece in range(8):
                for c in range(CHUNKS):
                    rows = turned[piece, c]
                    pieces[half * 8 + piece, c] = jnp.concatenate(
                        [rows[:, :BLOCK], rows[:, BLOCK:]], 0
                    ).astype(BF16)

    loads[1].wait()
    loads[2].wait()
    cut(grad, query, send_w)
    pl.semaphore_wait(barrier, len(OFFSETS))
    copies_t = send(lambda to: send_t.at[to], recv_t.at[me], t_send, t_recv)
    copies_w = send(lambda to: send_w.at[to], recv_w.at[me], w_send, w_recv)
    own_t = keep(send_t.at[me], recv_t.at[me], 2)
    own_w = keep(send_w.at[me], recv_w.at[me], 0)
    loads[3].wait()
    loads[4].wait()
    cut(key, value, send_u)
    copies_u = send(lambda to: send_u.at[to], recv_u.at[me], u_send, u_recv)
    own_u = keep(send_u.at[me], recv_u.at[me], 1)

    def slot_of(p, carry):
        found = jnp.int32(0)
        for s in range(SLOTS):
            found = jnp.where(table[s] == p, s, found)
        inverse[p] = found
        return carry

    for load in loads[5:]:
        load.wait()
    lax.fori_loop(0, SLOTS, slot_of, 0)
    q_out[...] = (grad[...].astype(F32) * conv[...].astype(F32)).astype(BF16)
    for c in range(CHUNKS):
        spec_v[c][SLOTS:] = jnp.zeros((LAG_BLOCKS - 1, ROWS, 3 * BLOCK), F32)
        spec_f[c][...] = jnp.zeros((LAG_BLOCKS, ROWS, 3 * BLOCK), F32)
    own_t.wait()
    own_w.wait()
    own_u.wait()
    for copy in copies_t:
        copy.wait_recv()

    order = [[jnp.zeros((16, BLOCK), F32) for _ in range(2)] for _ in range(LAG_BLOCKS)]
    for src in range(RANKS):
        first, shift = divmod(src * lags, BLOCK)
        packed = recv_t[src].astype(F32)
        for part in range(2):
            turn = (shift + 64 * part) % BLOCK
            rows = pltpu.roll(packed, turn, 1) if turn else packed
            inside = (lane >= shift) & (lane < shift + lags)
            order[first][part] = jnp.where(inside, rows, order[first][part])
            if shift + lags > BLOCK:
                order[first + 1][part] = jnp.where(lane < shift + lags - BLOCK, rows, order[first + 1][part])
    taps_in_order = jnp.concatenate([part for parts in order for part in parts], 0).astype(BF16)
    spec_h[...] = dot(taps_in_order, forward[:BLOCK]).reshape(LAG_BLOCKS, 32, SPAN)

    for start in range(0, RANKS, 4):
        for copy in copies_w[max(start - 1, 0):start + 3]:
            copy.wait_recv()
        batch = sources[start:start + 4]
        rows_w = jnp.concatenate([recv_w[src].reshape(CHUNKS * 16, BLOCK) for src in batch], 0)
        near = dot(rows_w, forward[:BLOCK]).reshape(4, CHUNKS, 2, ROWS, SPAN)
        later = dot(rows_w, forward[BLOCK:]).reshape(4, CHUNKS, 2, ROWS, SPAN)
        for i, src in enumerate(batch):
            for c in range(CHUNKS):
                spec_w[c][pl.ds(2 * src, 2), :, :SPAN] = near[i, c]
                spec_w[c][pl.ds(2 * src, 2), :, SPAN:] = later[i, c]

    def multiply(c):
        def window(p):
            slot = inverse[p]
            re = spec_w[c][slot, :, :BLOCK]
            im = spec_w[c][slot, :, BLOCK:SPAN]
            if p + 1 < SLOTS:
                after = inverse[p + 1]
                re = re + spec_w[c][after, :, SPAN:SPAN + BLOCK]
                im = im + spec_w[c][after, :, SPAN + BLOCK:]
            spec_v[c][p, :, :BLOCK] = re
            spec_v[c][p, :, BLOCK:SPAN] = im
            both = re + im
            spec_v[c][p, :, SPAN:] = both
            return re, im, both

        group = slice(c * ROWS, (c + 1) * ROWS)
        h = []
        for m in range(LAG_BLOCKS):
            re, im = spec_h[m, group, :BLOCK], spec_h[m, group, BLOCK:]
            h.append((re - im, re + im, re))
        windows = [window(p) for p in range(LAG_BLOCKS - 1)]
        for p in range(SLOTS):
            if p + LAG_BLOCKS - 1 < SLOTS:
                windows.append(window(p + LAG_BLOCKS - 1))
            d = None
            for m in range(min(LAG_BLOCKS, SLOTS - p)):
                v_re, v_im, v_both = windows[p + m]
                term = (h[m][0] * v_im, h[m][1] * v_re, h[m][2] * v_both)
                d = term if d is None else tuple(a + b for a, b in zip(d, term))
            windows[p] = None
            spec_d[c][p, :, :BLOCK] = d[2] - d[0]
            spec_d[c][p, :, BLOCK:] = d[2] - d[1]

    def invert(c):
        rows_d = jnp.concatenate([spec_d[c][table[s]] for s in range(SLOTS)], 0).astype(BF16)
        send_b[:, c] = dot(rows_d, back[...]).astype(BF16).reshape(RANKS, 2 * ROWS, BLOCK)

    copies_d = []
    for c in range(4):
        multiply(c)
        if c:
            invert(c - 1)
    invert(3)
    chunks = pl.ds(0, 4)
    copies_d += send(lambda to: send_b.at[to, chunks], out.at[me, chunks], d_send, d_recv)

    start = 0
    for count in BATCHES:
        for copy in copies_u[max(start - 1, 0):start + count - 1]:
            copy.wait_recv()
        batch = sources[start:start + count]
        start += count
        rows_u = jnp.concatenate([recv_u[src].reshape(CHUNKS * 16, BLOCK) for src in batch], 0)
        spec_u[:count] = dot(rows_u, forward[:BLOCK]).reshape(count, CHUNKS, 2, ROWS, SPAN)
        for c in range(CHUNKS):
            f = [[spec_f[c][m, :, part] for part in THIRDS] for m in range(LAG_BLOCKS)]
            for i, src in enumerate(batch):
                for b in range(2):
                    p = table[2 * src + b]
                    u_re, u_im = spec_u[i, c, b, :, :BLOCK], spec_u[i, c, b, :, BLOCK:]
                    u = (u_re - u_im, u_re + u_im, u_re)
                    for m in range(LAG_BLOCKS):
                        v_re, v_im, v_both = (spec_v[c][p + m, :, part] for part in THIRDS)
                        f[m][0] += u[0] * v_im
                        f[m][1] += u[1] * v_re
                        f[m][2] += u[2] * v_both
            for m in range(LAG_BLOCKS):
                for part, value_f in zip(THIRDS, f[m]):
                    spec_f[c][m, :, part] = value_f
    sums = jnp.concatenate([f[...].reshape(LAG_BLOCKS * ROWS, 3 * BLOCK) for f in spec_f], 0)
    last = sums[:, SPAN:]
    rows_f = jnp.concatenate([last - sums[:, :BLOCK], last - sums[:, BLOCK:SPAN]], 1).astype(BF16)
    scale = float((SLOTS * BLOCK) ** -0.5)
    lagged = (dot(rows_f, back[...]) * scale).reshape(CHUNKS, LAG_BLOCKS, ROWS, BLOCK)
    lag_rows = [
        [jnp.concatenate([lagged[2 * part, m], lagged[2 * part + 1, m]], 0) for part in range(2)]
        for m in range(LAG_BLOCKS)
    ]
    for to in range(RANKS):
        first, shift = divmod(to * lags, BLOCK)
        parts = []
        for part in range(2):
            turn = (64 * part - shift) % BLOCK
            rows = lag_rows[first][part]
            rows = pltpu.roll(rows, turn, 1) if turn else rows
            if shift + lags > BLOCK:
                later = pltpu.roll(lag_rows[first + 1][part], turn, 1)
                rows = jnp.where((lane & 63) < BLOCK - shift, rows, later)
            parts.append(rows)
        send_b[to, CHUNKS] = jnp.where(lower, parts[0], parts[1]).astype(BF16)
    copies_f = send(lambda to: send_b.at[to, CHUNKS], out.at[me, CHUNKS], f_send, f_recv)
    own_b = keep(send_b.at[me], out.at[me], 0)
    for copy in copies_t + copies_w + copies_u:
        copy.wait_send()
    own_b.wait()
    for copy in copies_d + copies_f:
        copy.wait()


def finish_kernel(key, value, pieces, q_in, q_out, k_out, v_out, f_out, k_rows, v_rows, f_rows, sems):
    copies = load_all(((q_in, q_out),), sems)
    unit = unit_matrix(BLOCK)
    channels = key.shape[1]
    packed = pieces[:, CHUNKS].astype(F32).reshape(RANKS * 16, BLOCK)
    upper = pltpu.roll(packed, 64, 1).reshape(RANKS, 16, BLOCK)
    both = jnp.stack([packed.reshape(RANKS, 16, BLOCK), upper], 1)
    f_rows[...] = flip(unit[:f_rows.shape[0]], both.reshape(channels, BLOCK).astype(BF16))
    copies += load_all(((f_rows, f_out),), sems.at[pl.ds(1, 1)])
    chunks = pieces[:, :CHUNKS].astype(F32).reshape(RANKS, CHUNKS, 2, ROWS, BLOCK)
    for b in range(2):
        rows = pl.ds(b * BLOCK, BLOCK)
        turned = flip(unit, chunks[:, :, b].reshape(channels, BLOCK).astype(BF16))
        k_rows[rows] = (turned * value[rows].astype(F32)).astype(BF16)
        v_rows[rows] = (turned * key[rows].astype(F32)).astype(BF16)
        copies += load_all(
            ((k_rows.at[rows], k_out.at[rows]), (v_rows.at[rows], v_out.at[rows])), sems.at[pl.ds(2 + 2 * b, 2)]
        )
    for copy in copies:
        copy.wait()


def on_device(out_grad, query_rows, key_rows, value_rows, conv_rows, long_filter, block_table):
    forward, back = tables()
    vmem = pl.BlockSpec(memory_space=pltpu.VMEM)
    units = (RANKS, CHUNKS + 1, 16, BLOCK)
    pieces_u = pltpu.VMEM((RANKS, CHUNKS, 16, BLOCK), BF16)
    dma = pltpu.SemaphoreType.DMA
    rows = jax.ShapeDtypeStruct(out_grad.shape, BF16)
    operands = (block_table, out_grad, query_rows, key_rows, value_rows, conv_rows, long_filter, forward, back)
    pieces, q_rows = pl.pallas_call(
        exchange_kernel,
        name="exchange",
        out_shape=(jax.ShapeDtypeStruct(units, BF16), rows),
        in_specs=[pl.BlockSpec(memory_space=pltpu.HBM)] * 9,
        out_specs=[vmem] * 2,
        scratch_shapes=[
            pltpu.SMEM((SLOTS,), jnp.int32),
            pltpu.SMEM((SLOTS,), jnp.int32),
            pltpu.VMEM(rows.shape, BF16),
            pltpu.VMEM(rows.shape, BF16),
            pltpu.VMEM(rows.shape, BF16),
            pltpu.VMEM(rows.shape, BF16),
            pltpu.VMEM(rows.shape, BF16),
            pltpu.VMEM(long_filter.shape, F32),
            pltpu.VMEM(forward.shape, BF16),
            pltpu.VMEM(back.shape, BF16),
            pltpu.VMEM((RANKS, 16, BLOCK), BF16),
            pltpu.VMEM((RANKS, 16, BLOCK), BF16),
            pieces_u,
            pieces_u,
            pieces_u,
            pieces_u,
            pltpu.VMEM(units, BF16),
            pltpu.VMEM((LAG_BLOCKS, 32, SPAN), F32),
            pltpu.VMEM((4, CHUNKS, 2, ROWS, SPAN), F32),
        ]
        + [pltpu.VMEM((SLOTS, ROWS, 2 * SPAN), F32)] * CHUNKS
        + [pltpu.VMEM((SLOTS + LAG_BLOCKS - 1, ROWS, 3 * BLOCK), F32)] * CHUNKS
        + [pltpu.VMEM((SLOTS, ROWS, SPAN), F32)] * CHUNKS
        + [pltpu.VMEM((LAG_BLOCKS, ROWS, 3 * BLOCK), F32)] * CHUNKS
        + [dma((9,))]
        + [dma((len(OFFSETS),))] * 10
        + [dma((3,))],
        compiler_params=pltpu.CompilerParams(
            collective_id=0, has_side_effects=True, vmem_limit_bytes=40 * 1024 * 1024
        ),
    )(*(pltpu.with_memory_space_constraint(x, pltpu.HBM) for x in operands))
    return pl.pallas_call(
        finish_kernel,
        name="finish",
        out_shape=(rows, rows, rows, jax.ShapeDtypeStruct(long_filter.shape, F32)),
        in_specs=[vmem] * 4,
        out_specs=[pl.BlockSpec(memory_space=pltpu.HBM)] * 4,
        scratch_shapes=[
            pltpu.VMEM(rows.shape, BF16), pltpu.VMEM(rows.shape, BF16), pltpu.VMEM(long_filter.shape, F32), dma((6,)),
        ],
        compiler_params=pltpu.CompilerParams(vmem_limit_bytes=40 * 1024 * 1024),
    )(key_rows, value_rows, pieces, q_rows)


def solution(mesh):
    rows = P("ctx", "tp")
    return jax.shard_map(
        on_device, mesh=mesh, in_specs=(rows,) * 6 + (P(),), out_specs=(rows,) * 4, check_vma=False
    )
```

```python
import functools

import jax
import jax.numpy as jnp
import numpy as np
from jax import lax
from jax.experimental import pallas as pl
from jax.experimental.pallas import tpu as pltpu
from jax.sharding import PartitionSpec as P

BLOCK = 128
LAG_BLOCKS = 6
SPAN = 2 * BLOCK
RANKS = 16
SLOTS = 2 * RANKS
MESH = pl.DeviceIdType.MESH
F32 = jnp.float32
BF16 = jnp.bfloat16
NT = (((1,), (1,)), ((), ()))


def tables():
    time = np.arange(SPAN)[:, None]
    bins = np.arange(BLOCK)[None, :] + 0.5
    angles = 2.0 * np.pi * time * bins / SPAN
    forward = np.concatenate([np.cos(angles), -np.sin(angles)], 1)
    back = np.concatenate([np.cos(angles[:BLOCK]).T, -np.sin(angles[:BLOCK]).T], 0) * (2.0 / SPAN)
    return jnp.asarray(forward, BF16), jnp.asarray(back, BF16)


def dot(left, right):
    return jnp.dot(left, right, preferred_element_type=F32)


def flip(eye, rows):
    return lax.dot_general(eye, rows, NT, preferred_element_type=F32)


def peer(me, offset):
    dx, dy, dc = offset
    x = lax.rem(lax.div(me, 4) + dx, 4)
    y = lax.rem(lax.rem(lax.div(me, 2), 2) + dy, 2)
    c = lax.rem(lax.rem(me, 2) + dc, 2)
    return (x * 2 + y) * 2 + c


OFFSETS = (
    (2, 1, 1), (2, 1, 0), (1, 1, 1), (3, 1, 0), (3, 1, 1), (1, 1, 0), (2, 0, 1), (0, 1, 0),
    (0, 1, 1), (2, 0, 0), (1, 0, 1), (3, 0, 0), (3, 0, 1), (1, 0, 0), (0, 0, 1),
)


CHUNKS = 4
ROWS = 8
BATCHES = (4, 4, 4, 3, 1)
THIRDS = tuple(slice(i * BLOCK, (i + 1) * BLOCK) for i in range(3))


def load_all(pairs, sems):
    loads = []
    for i, (source, target) in enumerate(pairs):
        load = pltpu.make_async_copy(source, target, sems.at[i])
        load.start()
        loads.append(load)
    return loads


def unit_matrix(size):
    row = lax.broadcasted_iota(jnp.int32, (size, size), 0)
    column = lax.broadcasted_iota(jnp.int32, (size, size), 1)
    return jnp.where(row == column, 1.0, 0.0).astype(BF16)


def exchange_kernel(
    table_in, grad_in, query_in, key_in, value_in, conv_in, taps_in, forward_in, back_in, out, q_out,
    table, inverse, grad, query, key, value, conv, taps, forward, back,
    send_t, recv_t, send_w, recv_w, send_u, recv_u, send_b, spec_h, spec_u,
    spec_w0, spec_w1, spec_w2, spec_w3, spec_v0, spec_v1, spec_v2, spec_v3,
    spec_d0, spec_d1, spec_d2, spec_d3, spec_f0, spec_f1, spec_f2, spec_f3,
    load_sems, t_send, t_recv, w_send, w_recv, u_send, u_recv, d_send, d_recv, f_send, f_recv, own_sems,
):
    spec_w = (spec_w0, spec_w1, spec_w2, spec_w3)
    spec_v = (spec_v0, spec_v1, spec_v2, spec_v3)
    spec_d = (spec_d0, spec_d1, spec_d2, spec_d3)
    spec_f = (spec_f0, spec_f1, spec_f2, spec_f3)
    me = lax.axis_index("ctx")
    peers = [peer(me, offset) for offset in OFFSETS]
    barrier = pltpu.get_barrier_semaphore()
    for to in peers:
        pl.semaphore_signal(barrier, inc=1, device_id={"ctx": to}, device_id_type=MESH)
    sources = [me] + [peer(me, ((4 - dx) % 4, dy, dc)) for dx, dy, dc in OFFSETS]
    loads = load_all(
        ((taps_in, taps), (grad_in, grad), (query_in, query), (key_in, key), (value_in, value),
         (forward_in, forward), (back_in, back), (table_in, table), (conv_in, conv)),
        load_sems,
    )

    def send(source, target, send_sems, recv_sems):
        copies = []
        for i, to in enumerate(peers):
            copy = pltpu.make_async_remote_copy(
                source(to), target, send_sems.at[i], recv_sems.at[i],
                device_id={"ctx": to}, device_id_type=MESH,
            )
            copy.start()
            copies.append(copy)
        return copies

    def keep(source, target, i):
        copy = pltpu.make_async_copy(source, target, own_sems.at[i])
        copy.start()
        return copy

    unit = unit_matrix(SPAN)
    lane = lax.broadcasted_iota(jnp.int32, (16, BLOCK), 1)
    lower = lane < 64
    lags = taps.shape[0]
    loads[0].wait()
    padded = jnp.concatenate([taps[...].astype(BF16), jnp.zeros((BLOCK - lags, taps.shape[1]), BF16)], 0)
    for half in range(2):
        turned = flip(unit, padded[:, half * SPAN:(half + 1) * SPAN])
        for piece in range(8):
            rows = turned[piece * 32:(piece + 1) * 32]
            packed = jnp.where(lower, rows[:16], pltpu.roll(rows[16:], 64, 1))
            send_t[half * 8 + piece] = packed.astype(BF16)

    def cut(left, right, pieces):
        product = (left[...].astype(F32) * right[...].astype(F32)).astype(BF16)
        for half in range(2):
            turned = flip(unit, product[:, half * SPAN:(half + 1) * SPAN]).reshape(8, CHUNKS, ROWS, SPAN)
            for piece in range(8):
                for c in range(CHUNKS):
                    rows = turned[piece, c]
                    pieces[half * 8 + piece, c] = jnp.concatenate(
                        [rows[:, :BLOCK], rows[:, BLOCK:]], 0
                    ).astype(BF16)

    loads[1].wait()
    loads[2].wait()
    cut(grad, query, send_w)
    pl.semaphore_wait(barrier, len(OFFSETS))
    copies_t = send(lambda to: send_t.at[to], recv_t.at[me], t_send, t_recv)
    copies_w = send(lambda to: send_w.at[to], recv_w.at[me], w_send, w_recv)
    own_t = keep(send_t.at[me], recv_t.at[me], 2)
    own_w = keep(send_w.at[me], recv_w.at[me], 0)
    loads[3].wait()
    loads[4].wait()
    cut(key, value, send_u)
    copies_u = send(lambda to: send_u.at[to], recv_u.at[me], u_send, u_recv)
    own_u = keep(send_u.at[me], recv_u.at[me], 1)

    def slot_of(p, carry):
        found = jnp.int32(0)
        for s in range(SLOTS):
            found = jnp.where(table[s] == p, s, found)
        inverse[p] = found
        return carry

    for load in loads[5:]:
        load.wait()
    lax.fori_loop(0, SLOTS, slot_of, 0)
    q_out[...] = (grad[...].astype(F32) * conv[...].astype(F32)).astype(BF16)
    for c in range(CHUNKS):
        spec_v[c][SLOTS:] = jnp.zeros((LAG_BLOCKS - 1, ROWS, 3 * BLOCK), F32)
        spec_f[c][...] = jnp.zeros((LAG_BLOCKS, ROWS, 3 * BLOCK), F32)
    own_t.wait()
    own_w.wait()
    own_u.wait()
    for copy in copies_t:
        copy.wait_recv()

    order = [[jnp.zeros((16, BLOCK), F32) for _ in range(2)] for _ in range(LAG_BLOCKS)]
    for src in range(RANKS):
        first, shift = divmod(src * lags, BLOCK)
        packed = recv_t[src].astype(F32)
        for part in range(2):
            turn = (shift + 64 * part) % BLOCK
            rows = pltpu.roll(packed, turn, 1) if turn else packed
            inside = (lane >= shift) & (lane < shift + lags)
            order[first][part] = jnp.where(inside, rows, order[first][part])
            if shift + lags > BLOCK:
                order[first + 1][part] = jnp.where(lane < shift + lags - BLOCK, rows, order[first + 1][part])
    taps_in_order = jnp.concatenate([part for parts in order for part in parts], 0).astype(BF16)
    spec_h[...] = dot(taps_in_order, forward[:BLOCK]).reshape(LAG_BLOCKS, 32, SPAN)

    for start in range(0, RANKS, 4):
        for copy in copies_w[max(start - 1, 0):start + 3]:
            copy.wait_recv()
        batch = sources[start:start + 4]
        rows_w = jnp.concatenate([recv_w[src].reshape(CHUNKS * 16, BLOCK) for src in batch], 0)
        near = dot(rows_w, forward[:BLOCK]).reshape(4, CHUNKS, 2, ROWS, SPAN)
        later = dot(rows_w, forward[BLOCK:]).reshape(4, CHUNKS, 2, ROWS, SPAN)
        for i, src in enumerate(batch):
            for c in range(CHUNKS):
                spec_w[c][pl.ds(2 * src, 2), :, :SPAN] = near[i, c]
                spec_w[c][pl.ds(2 * src, 2), :, SPAN:] = later[i, c]

    def multiply(c):
        def window(p):
            slot = inverse[p]
            re = spec_w[c][slot, :, :BLOCK]
            im = spec_w[c][slot, :, BLOCK:SPAN]
            if p + 1 < SLOTS:
                after = inverse[p + 1]
                re = re + spec_w[c][after, :, SPAN:SPAN + BLOCK]
                im = im + spec_w[c][after, :, SPAN + BLOCK:]
            spec_v[c][p, :, :BLOCK] = re
            spec_v[c][p, :, BLOCK:SPAN] = im
            both = re + im
            spec_v[c][p, :, SPAN:] = both
            return re, im, both

        group = slice(c * ROWS, (c + 1) * ROWS)
        h = []
        for m in range(LAG_BLOCKS):
            re, im = spec_h[m, group, :BLOCK], spec_h[m, group, BLOCK:]
            h.append((re - im, re + im, re))
        windows = [window(p) for p in range(LAG_BLOCKS - 1)]
        for p in range(SLOTS):
            if p + LAG_BLOCKS - 1 < SLOTS:
                windows.append(window(p + LAG_BLOCKS - 1))
            d = None
            for m in range(min(LAG_BLOCKS, SLOTS - p)):
                v_re, v_im, v_both = windows[p + m]
                term = (h[m][0] * v_im, h[m][1] * v_re, h[m][2] * v_both)
                d = term if d is None else tuple(a + b for a, b in zip(d, term))
            windows[p] = None
            spec_d[c][p, :, :BLOCK] = d[2] - d[0]
            spec_d[c][p, :, BLOCK:] = d[2] - d[1]

    def invert(c):
        rows_d = jnp.concatenate([spec_d[c][table[s]] for s in range(SLOTS)], 0).astype(BF16)
        send_b[:, c] = dot(rows_d, back[...]).astype(BF16).reshape(RANKS, 2 * ROWS, BLOCK)

    copies_d = []
    for c in range(4):
        multiply(c)
        if c:
            invert(c - 1)
    invert(3)
    chunks = pl.ds(0, 4)
    copies_d += send(lambda to: send_b.at[to, chunks], out.at[me, chunks], d_send, d_recv)

    start = 0
    for count in BATCHES:
        for copy in copies_u[max(start - 1, 0):start + count - 1]:
            copy.wait_recv()
        batch = sources[start:start + count]
        start += count
        rows_u = jnp.concatenate([recv_u[src].reshape(CHUNKS * 16, BLOCK) for src in batch], 0)
        spec_u[:count] = dot(rows_u, forward[:BLOCK]).reshape(count, CHUNKS, 2, ROWS, SPAN)
        for c in range(CHUNKS):
            f = [[spec_f[c][m, :, part] for part in THIRDS] for m in range(LAG_BLOCKS)]
            for i, src in enumerate(batch):
                for b in range(2):
                    p = table[2 * src + b]
                    u_re, u_im = spec_u[i, c, b, :, :BLOCK], spec_u[i, c, b, :, BLOCK:]
                    u = (u_re - u_im, u_re + u_im, u_re)
                    for m in range(LAG_BLOCKS):
                        v_re, v_im, v_both = (spec_v[c][p + m, :, part] for part in THIRDS)
                        f[m][0] += u[0] * v_im
                        f[m][1] += u[1] * v_re
                        f[m][2] += u[2] * v_both
            for m in range(LAG_BLOCKS):
                for part, value_f in zip(THIRDS, f[m]):
                    spec_f[c][m, :, part] = value_f
    sums = jnp.concatenate([f[...].reshape(LAG_BLOCKS * ROWS, 3 * BLOCK) for f in spec_f], 0)
    last = sums[:, SPAN:]
    rows_f = jnp.concatenate([last - sums[:, :BLOCK], last - sums[:, BLOCK:SPAN]], 1).astype(BF16)
    scale = float((SLOTS * BLOCK) ** -0.5)
    lagged = (dot(rows_f, back[...]) * scale).reshape(CHUNKS, LAG_BLOCKS, ROWS, BLOCK)
    lag_rows = [
        [jnp.concatenate([lagged[2 * part, m], lagged[2 * part + 1, m]], 0) for part in range(2)]
        for m in range(LAG_BLOCKS)
    ]
    for to in range(RANKS):
        first, shift = divmod(to * lags, BLOCK)
        parts = []
        for part in range(2):
            turn = (64 * part - shift) % BLOCK
            rows = lag_rows[first][part]
            rows = pltpu.roll(rows, turn, 1) if turn else rows
            if shift + lags > BLOCK:
                later = pltpu.roll(lag_rows[first + 1][part], turn, 1)
                rows = jnp.where((lane & 63) < BLOCK - shift, rows, later)
            parts.append(rows)
        send_b[to, CHUNKS] = jnp.where(lower, parts[0], parts[1]).astype(BF16)
    copies_f = send(lambda to: send_b.at[to, CHUNKS], out.at[me, CHUNKS], f_send, f_recv)
    own_b = keep(send_b.at[me], out.at[me], 0)
    own_b.wait()
    for copy in copies_t + copies_w + copies_u + copies_d + copies_f:
        copy.wait_send()
    for copy in copies_d + copies_f[::-1]:
        copy.wait_recv()


def finish_kernel(key, value, pieces, q_in, q_out, k_out, v_out, f_out, k_rows, v_rows, f_rows, sems):
    copies = load_all(((q_in, q_out),), sems)
    unit = unit_matrix(BLOCK)
    channels = key.shape[1]
    packed = pieces[:, CHUNKS].astype(F32).reshape(RANKS * 16, BLOCK)
    upper = pltpu.roll(packed, 64, 1).reshape(RANKS, 16, BLOCK)
    both = jnp.stack([packed.reshape(RANKS, 16, BLOCK), upper], 1)
    f_rows[...] = flip(unit[:f_rows.shape[0]], both.reshape(channels, BLOCK).astype(BF16))
    copies += load_all(((f_rows, f_out),), sems.at[pl.ds(1, 1)])
    chunks = pieces[:, :CHUNKS].astype(F32).reshape(RANKS, CHUNKS, 2, ROWS, BLOCK)
    for b in range(2):
        rows = pl.ds(b * BLOCK, BLOCK)
        turned = flip(unit, chunks[:, :, b].reshape(channels, BLOCK).astype(BF16))
        k_rows[rows] = (turned * value[rows].astype(F32)).astype(BF16)
        v_rows[rows] = (turned * key[rows].astype(F32)).astype(BF16)
        copies += load_all(
            ((k_rows.at[rows], k_out.at[rows]), (v_rows.at[rows], v_out.at[rows])), sems.at[pl.ds(2 + 2 * b, 2)]
        )
    for copy in copies:
        copy.wait()


def on_device(out_grad, query_rows, key_rows, value_rows, conv_rows, long_filter, block_table):
    forward, back = tables()
    vmem = pl.BlockSpec(memory_space=pltpu.VMEM)
    units = (RANKS, CHUNKS + 1, 16, BLOCK)
    pieces_u = pltpu.VMEM((RANKS, CHUNKS, 16, BLOCK), BF16)
    dma = pltpu.SemaphoreType.DMA
    rows = jax.ShapeDtypeStruct(out_grad.shape, BF16)
    operands = (block_table, out_grad, query_rows, key_rows, value_rows, conv_rows, long_filter, forward, back)
    pieces, q_rows = pl.pallas_call(
        exchange_kernel,
        name="exchange",
        out_shape=(jax.ShapeDtypeStruct(units, BF16), rows),
        in_specs=[pl.BlockSpec(memory_space=pltpu.HBM)] * 9,
        out_specs=[vmem] * 2,
        scratch_shapes=[
            pltpu.SMEM((SLOTS,), jnp.int32),
            pltpu.SMEM((SLOTS,), jnp.int32),
            pltpu.VMEM(rows.shape, BF16),
            pltpu.VMEM(rows.shape, BF16),
            pltpu.VMEM(rows.shape, BF16),
            pltpu.VMEM(rows.shape, BF16),
            pltpu.VMEM(rows.shape, BF16),
            pltpu.VMEM(long_filter.shape, F32),
            pltpu.VMEM(forward.shape, BF16),
            pltpu.VMEM(back.shape, BF16),
            pltpu.VMEM((RANKS, 16, BLOCK), BF16),
            pltpu.VMEM((RANKS, 16, BLOCK), BF16),
            pieces_u,
            pieces_u,
            pieces_u,
            pieces_u,
            pltpu.VMEM(units, BF16),
            pltpu.VMEM((LAG_BLOCKS, 32, SPAN), F32),
            pltpu.VMEM((4, CHUNKS, 2, ROWS, SPAN), F32),
        ]
        + [pltpu.VMEM((SLOTS, ROWS, 2 * SPAN), F32)] * CHUNKS
        + [pltpu.VMEM((SLOTS + LAG_BLOCKS - 1, ROWS, 3 * BLOCK), F32)] * CHUNKS
        + [pltpu.VMEM((SLOTS, ROWS, SPAN), F32)] * CHUNKS
        + [pltpu.VMEM((LAG_BLOCKS, ROWS, 3 * BLOCK), F32)] * CHUNKS
        + [dma((9,))]
        + [dma((len(OFFSETS),))] * 10
        + [dma((3,))],
        compiler_params=pltpu.CompilerParams(
            collective_id=0, has_side_effects=True, vmem_limit_bytes=40 * 1024 * 1024
        ),
    )(*(pltpu.with_memory_space_constraint(x, pltpu.HBM) for x in operands))
    return pl.pallas_call(
        finish_kernel,
        name="finish",
        out_shape=(rows, rows, rows, jax.ShapeDtypeStruct(long_filter.shape, F32)),
        in_specs=[vmem] * 4,
        out_specs=[pl.BlockSpec(memory_space=pltpu.HBM)] * 4,
        scratch_shapes=[
            pltpu.VMEM(rows.shape, BF16), pltpu.VMEM(rows.shape, BF16), pltpu.VMEM(long_filter.shape, F32), dma((6,)),
        ],
        compiler_params=pltpu.CompilerParams(vmem_limit_bytes=40 * 1024 * 1024),
    )(key_rows, value_rows, pieces, q_rows)


def solution(mesh):
    rows = P("ctx", "tp")
    return jax.shard_map(
        on_device, mesh=mesh, in_specs=(rows,) * 6 + (P(),), out_specs=(rows,) * 4, check_vma=False
    )
```
